32 devices in a mesh: seq: 16 (over z, y, x), chan: 2 (over core).
Axes of the slice: x: 2, y: 2, z: 4, core: 2. Of those that a mesh axis runs over, the one named last changes fastest.
Arguments:
- tokens: bfloat16 [2048, 4096], P('seq', 'chan'), may hold values from -6 to 6
- conv_taps: float32 [4, 4096], P(None, 'chan'), may hold values from -12 to 12
- log_rate: float32 [4096], P('chan'), may hold values from 1.953125e-05 to 0.034
- rotation: float32 [4096], P('chan'), may hold values from 0 to 0.2
- in_proj: bfloat16 [64, 64, 128], P('chan'), may hold values from -0.75 to 0.75
- out_proj: bfloat16 [64, 64, 128], P('chan'), may hold values from -0.5 to 0.5
- skip_gain: float32 [4096], P('chan'), may hold values from 0.25 to 1.5
- norm_gain: float32 [4096], P('chan'), may hold values from 0.25 to 1.75
- retention: float32 [2048], P('seq'), may hold values from 0.5 to 1
- cotangent: bfloat16 [2048, 4096], P('seq', 'chan'), may hold values from -6 to 6
Outputs:
- normed: bfloat16 [2048, 4096], P('seq', 'chan')
- tokens_grad: bfloat16 [2048, 4096], P('seq', 'chan')
- in_grad: float32 [64, 64, 128], P('chan')
- out_grad: float32 [64, 64, 128], P('chan')
- taps_grad: float32 [4, 4096], P(None, 'chan')
The draws below stay inside these ranges and needn't reach their ends.
All inputs are finite; a program needn't handle non-finite values.
Results may differ from the reference program's by a relative error of at most 0.011.
Values may be sent and summed in bfloat16 or wider, within the bound.
A program may use at most 128 MiB of HBM per device.

```python
import jax
import jax.numpy as jnp
from jax import lax

D = 4096
HW = 64
STATE = 64
KW = 4
TOK_DEV = 128
HEADS = 64
STATES = 4096
TOKENS = 2048


def draw_conv_taps(key, part):
    first_key, second_key = jax.random.split(key)
    channels = jnp.arange(D, dtype=jnp.float32)
    rising = jnp.exp(0.5 * jnp.log(3.0) * channels / D)
    jitter = jnp.exp(jax.random.uniform(second_key, (D,), jnp.float32, jnp.log(0.3), jnp.log(3.0)))
    base = jnp.clip(jax.random.normal(first_key, (KW, D), jnp.float32), -4.0, 4.0)
    return 0.5 * base * rising[None, :] * jitter[None, :]


def draw_log_rate(key, part):
    first_key, second_key, third_key = jax.random.split(key, 3)
    slow_flag = jax.random.randint(first_key, (STATES,), 0, 2) > 0
    slow_rate = jnp.exp(jax.random.uniform(second_key, (STATES,), jnp.float32, jnp.log(0.05), jnp.log(2.0))) / TOKENS
    fast_rate = jnp.exp(jax.random.uniform(third_key, (STATES,), jnp.float32, jnp.log(1.0 / 50.0), jnp.log(1.0 / 30.0)))
    return jnp.where(slow_flag, slow_rate, fast_rate)


def draw_retention(key, part):
    first_key, second_key = jax.random.split(key)
    hits = jax.random.randint(first_key, (TOKENS,), 0, TOKENS) < 12
    dropped = jax.random.uniform(second_key, (TOKENS,), jnp.float32, 0.5, 0.8)
    return jnp.where(hits, dropped, 1.0)


def block_scale(rng, extent, cuts, low, largest):
    gain = 1.0
    for position, parts in cuts:
        draws = jax.random.uniform(jax.random.fold_in(jax.random.fold_in(rng, 6), position), (parts,), jnp.float32, low / len(cuts), largest / len(cuts))
        gain = gain * jnp.repeat(jnp.exp(draws), extent[position] // parts).reshape((-1,) + (1,) * (len(extent) - 1 - position))
    return gain


def gaussian(stream_key, shape, scale, bound, shards=(), kind=jnp.bfloat16):
    result = scale * jax.random.normal(stream_key, shape, jnp.float32)
    if shards:
        result = result * block_scale(stream_key, shape, shards, -0.22, 0.18)
    return jnp.clip(result, -bound, bound).astype(kind)


def setup_inputs(seed: int = 0) -> dict:
    arg_keys = jax.random.split(jax.random.key(seed), 11)
    return {
        "tokens": gaussian(arg_keys[0], (TOKENS, D), 1.0, 6.0, ((0, 16), (1, 2))),
        "conv_taps": draw_conv_taps(jax.random.fold_in(arg_keys[10], 71), 0),
        "log_rate": draw_log_rate(jax.random.fold_in(arg_keys[10], 71), 0),
        "rotation": jnp.clip(0.2 * jax.random.uniform(arg_keys[3], (STATES,), jnp.float32) ** block_scale(arg_keys[3], (STATES,), ((0, 2),), -0.2, 0.2), 0.0, 0.2),
        "in_proj": gaussian(arg_keys[4], (HEADS, HW, 2 * STATE), HW ** -0.5, 0.75, ((0, 2),)),
        "out_proj": gaussian(arg_keys[5], (HEADS, HW, 2 * STATE), (2 * STATE) ** -0.5, 0.5, ((0, 2),)),
        "skip_gain": jnp.clip(0.25 + 1.25 * jax.random.uniform(arg_keys[6], (D,), jnp.float32) ** block_scale(arg_keys[6], (D,), ((0, 2),), -0.2, 0.2), 0.25, 1.5),
        "norm_gain": jnp.clip(1.0 + 0.15 * jax.random.normal(arg_keys[7], (D,), jnp.float32), 0.25, 1.75),
        "retention": draw_retention(jax.random.fold_in(arg_keys[10], 71), 0),
        "cotangent": gaussian(arg_keys[9], (TOKENS, D), 1.0, 6.0, ((0, 16), (1, 2))),
    }


def reference(tokens, conv_taps, log_rate, rotation, in_proj, out_proj, skip_gain, norm_gain, retention, cotangent):
    block_total = TOKENS // TOK_DEV
    decay_mag = jnp.exp(-log_rate)
    lam_re = decay_mag * jnp.cos(rotation)
    lam_im = decay_mag * jnp.sin(rotation)
    in_scale = jnp.sqrt(-jnp.expm1(-2.0 * log_rate))
    in_wide = in_proj.astype(jnp.float32)
    out_wide = out_proj.astype(jnp.float32)
    token_blocks = tokens.reshape(block_total, TOK_DEV, D)
    keep_blocks = retention.reshape(block_total, TOK_DEV)
    cot_blocks = cotangent.reshape(block_total, TOK_DEV, D)
    highest = lax.Precision.HIGHEST

    def convolve(block, lead_rows):
        padded = jnp.concatenate([lead_rows, block.astype(jnp.float32)], axis=0)
        summed = conv_taps[0][None, :] * padded[KW - 1:]
        for offset in range(1, KW):
            summed = summed + conv_taps[offset][None, :] * padded[KW - 1 - offset:KW - 1 - offset + TOK_DEV]
        return (summed.astype(jnp.bfloat16), padded)

    def drive(mixed_in):
        projected = jnp.einsum('thc,hck->thk', mixed_in.astype(jnp.float32).reshape(TOK_DEV, HEADS, HW), in_wide, precision=highest)
        drive_re = projected[:, :, :STATE].reshape(TOK_DEV, STATES) * in_scale
        drive_im = projected[:, :, STATE:].reshape(TOK_DEV, STATES) * in_scale
        return (drive_re, drive_im)

    def states(start_re, start_im, drive_re, drive_im, keep):

        def advance(carried, item):
            old_re, old_im = carried
            in_re, in_im, keep_now = item
            new_re = keep_now * (lam_re * old_re - lam_im * old_im) + in_re
            new_im = keep_now * (lam_re * old_im + lam_im * old_re) + in_im
            return ((new_re, new_im), (new_re, new_im))
        return lax.scan(advance, (start_re, start_im), (drive_re, drive_im, keep))[1]

    def readout(seq_re, seq_im, mixed_in):
        state_bf = jnp.concatenate([seq_re.reshape(TOK_DEV, HEADS, STATE), seq_im.reshape(TOK_DEV, HEADS, STATE)], axis=2).astype(jnp.bfloat16)
        mixed = jnp.einsum('thk,hck->thc', state_bf.astype(jnp.float32), out_wide, precision=highest).reshape(TOK_DEV, D)
        mixed = mixed + skip_gain * mixed_in.astype(jnp.float32)
        return (state_bf, mixed)

    def forward_step(carried, item):
        start_re, start_im, lead_rows = carried
        block, keep = item
        mixed_in, padded = convolve(block, lead_rows)
        drive_re, drive_im = drive(mixed_in)
        seq_re, seq_im = states(start_re, start_im, drive_re, drive_im, keep)
        state_bf, mixed = readout(seq_re, seq_im, mixed_in)
        inverse = lax.rsqrt(lax.optimization_barrier(jnp.mean(mixed * mixed, axis=1)) + 1e-06)
        normed = (mixed * inverse[:, None] * norm_gain).astype(jnp.bfloat16)
        return ((seq_re[-1], seq_im[-1], padded[TOK_DEV:]), (normed, start_re, start_im, lead_rows))
    zero_state = jnp.zeros((STATES,), jnp.float32)
    zero_lead = jnp.zeros((KW - 1, D), jnp.float32)
    normed_blocks, starts_re, starts_im, leads = lax.scan(forward_step, (zero_state, zero_state, zero_lead), (token_blocks, keep_blocks))[1]

    def backward_step(carried, item):
        pend_re, pend_im, trail_rows, in_acc, out_acc, taps_acc = carried
        block, keep, cot, start_re, start_im, lead_rows = item
        mixed_in, padded = convolve(block, lead_rows)
        drive_re, drive_im = drive(mixed_in)
        seq_re, seq_im = states(start_re, start_im, drive_re, drive_im, keep)
        state_bf, mixed = readout(seq_re, seq_im, mixed_in)
        inverse = lax.rsqrt(lax.optimization_barrier(jnp.mean(mixed * mixed, axis=1)) + 1e-06)
        scaled = cot.astype(jnp.float32) * norm_gain
        dots = lax.optimization_barrier(jnp.sum(scaled * mixed, axis=1))
        mixed_grad = inverse[:, None] * (scaled - mixed * (inverse * inverse * dots / D)[:, None])
        grad_bf = mixed_grad.astype(jnp.bfloat16).reshape(TOK_DEV, HEADS, HW).astype(jnp.float32)
        state_grad = jnp.einsum('thc,hck->thk', grad_bf, out_wide, precision=highest)
        out_acc = out_acc + jnp.einsum('thc,thk->hck', grad_bf, state_bf.astype(jnp.float32), precision=highest)

        def retreat(pending, item_now):
            pending_re, pending_im = pending
            grad_re, grad_im, keep_now = item_now
            adj_re = grad_re + pending_re
            adj_im = grad_im + pending_im
            next_re = keep_now * (lam_re * adj_re + lam_im * adj_im)
            next_im = keep_now * (lam_re * adj_im - lam_im * adj_re)
            return ((next_re, next_im), (adj_re, adj_im))
        grad_re = state_grad[:, :, :STATE].reshape(TOK_DEV, STATES)
        grad_im = state_grad[:, :, STATE:].reshape(TOK_DEV, STATES)
        (pend_re, pend_im), (adj_re, adj_im) = lax.scan(retreat, (pend_re, pend_im), (grad_re, grad_im, keep), reverse=True)
        drive_grad = jnp.concatenate([(in_scale * adj_re).reshape(TOK_DEV, HEADS, STATE), (in_scale * adj_im).reshape(TOK_DEV, HEADS, STATE)], axis=2).astype(jnp.bfloat16).astype(jnp.float32)
        in_acc = in_acc + jnp.einsum('thc,thk->hck', mixed_in.astype(jnp.float32).reshape(TOK_DEV, HEADS, HW), drive_grad, precision=highest)
        input_grad = jnp.einsum('thk,hck->thc', drive_grad, in_wide, precision=highest).reshape(TOK_DEV, D) + skip_gain * mixed_grad
        tail = jnp.concatenate([input_grad, trail_rows], axis=0)
        grad_tokens = conv_taps[0][None, :] * tail[:TOK_DEV]
        for offset in range(1, KW):
            grad_tokens = grad_tokens + conv_taps[offset][None, :] * tail[offset:offset + TOK_DEV]
        taps_term = jnp.stack([lax.optimization_barrier(jnp.sum(input_grad * padded[KW - 1 - offset:KW - 1 - offset + TOK_DEV], axis=0)) for offset in range(KW)])
        taps_acc = taps_acc + taps_term
        return ((pend_re, pend_im, input_grad[:KW - 1], in_acc, out_acc, taps_acc), grad_tokens.astype(jnp.bfloat16))
    zero_proj = jnp.zeros((HEADS, HW, 2 * STATE), jnp.float32)
    zero_taps = jnp.zeros((KW, D), jnp.float32)
    init = (zero_state, zero_state, zero_lead, zero_proj, zero_proj, zero_taps)
    final, grad_blocks = lax.scan(backward_step, init, (token_blocks, keep_blocks, cot_blocks, starts_re, starts_im, leads), reverse=True)
    return (normed_blocks.reshape(TOKENS, D), grad_blocks.reshape(TOKENS, D), final[3], final[4], final[5])
```

```python
import functools

import jax
import jax.numpy as jnp
from jax import lax
from jax.experimental import pallas as pl
from jax.experimental.pallas import tpu as pltpu
from jax.sharding import PartitionSpec as P

LANES = 128
F32 = jnp.float32
BF16 = jnp.bfloat16


def cmul(a, b):
    return a[0] * b[0] - a[1] * b[1], a[0] * b[1] + a[1] * b[0]


def cpow(base, exponent):
    result = None
    while exponent:
        if exponent & 1:
            result = base if result is None else cmul(result, base)
        exponent >>= 1
        if exponent:
            base = cmul(base, base)
    return result


def dot(a, b, ca, cb):
    return lax.dot_general(a, b, (((ca,), (cb,)), ((), ())), preferred_element_type=F32)


def scale_of(rate):
    sq = rate * rate
    sinh = rate * (1 + sq / 6 * (1 + sq / 20 * (1 + sq / 42 * (1 + sq / 72))))
    return jnp.sqrt(2.0 * jnp.exp(-rate) * sinh)


def kernel(dims, *refs):
    (tok, taps, rate_row, rate_t, rot_t, win, wout, skip, gain, cot, keep,
     normed_o, tg_o, in_o, out_o, taps_o,
     pad, mixed_in, d_re, d_im, s_bf, mixed, g_bf, ig, w_in, w_out, scale_row, tsc, halo, ihalo,
     nbuf, fb1, fb2, bb1, bb2, msg_o, rs1_o, mid_o, rs2_o, res_o,
     msg_i, rs1_i, mid_i, rs2_i, res_i,
     s_halo, s_norm, s_f1, s_f2, s_b1, s_b2, s_o1, s_o2, s_o3, s_o4, s_i1, s_i2, s_i3, s_i4) = refs
    T, W, NP, PP, KW, HW, G, Z, C, NSEQ, ROWS, RO, RI = dims
    me = lax.axis_index("seq")
    core = lax.axis_index("chan")
    gi = lax.rem(me, G)
    zi = me // G

    def plane(i):
        return {"seq": zi * G + lax.rem(gi + i, G)}

    def along(i):
        return {"seq": lax.rem(zi + i, Z) * G + gi}

    def other(i):
        return {"chan": lax.rem(core + i, C)}

    nxt = {"seq": lax.rem(me + 1, NSEQ)}
    prv = {"seq": lax.rem(me + NSEQ - 1, NSEQ)}

    peers = [plane(i) for i in range(1, G)] + [along(i) for i in range(1, Z)]
    peers += [other(i) for i in range(1, C)] + [nxt, prv]
    barrier = pltpu.get_barrier_semaphore()
    for peer in peers:
        pl.semaphore_signal(barrier, inc=1, device_id=peer, device_id_type=pl.DeviceIdType.MESH)

    def remote(src, dst, sems, i, device):
        return pltpu.make_async_remote_copy(
            src_ref=src, dst_ref=dst, send_sem=sems.at[0, i], recv_sem=sems.at[1, i],
            device_id=device, device_id_type=pl.DeviceIdType.MESH,
        )

    def loop(count, body):
        lax.fori_loop(0, count, lambda i, _: (body(i), None)[1], None)

    def cols(j, width=LANES):
        return pl.ds(pl.multiple_of(j * width, width), width)

    low = lax.broadcasted_iota(jnp.int32, (HW, LANES), 1) < HW

    def pair_weights(src, dst):
        def one(j):
            a = src[2 * j].astype(F32)
            b = src[2 * j + 1].astype(F32)
            ar = pltpu.roll(a, HW, 1)
            br = pltpu.roll(b, HW, 1)
            dst[j, :HW, :LANES] = jnp.where(low, a, 0.0).astype(BF16)
            dst[j, HW:, :LANES] = jnp.where(low, 0.0, br).astype(BF16)
            dst[j, :HW, LANES:] = jnp.where(low, ar, 0.0).astype(BF16)
            dst[j, HW:, LANES:] = jnp.where(low, 0.0, b).astype(BF16)
        loop(NP, one)

    def unpair(r):
        top_re, top_im = r[:HW, :LANES], r[:HW, LANES:]
        bot_re, bot_im = r[HW:, :LANES], r[HW:, LANES:]
        a = jnp.where(low, top_re, pltpu.roll(top_im, HW, 1))
        b = jnp.where(low, pltpu.roll(bot_re, HW, 1), bot_im)
        return a, b

    pl.semaphore_wait(barrier, len(peers))
    send_halo = remote(tok.at[pl.ds(T - 16, 16)], halo, s_halo, 0, nxt)
    send_halo.start()

    pair_weights(win, w_in)
    pair_weights(wout, w_out)
    if PP != NP:
        d_re[...] = jnp.zeros_like(d_re)
        d_im[...] = jnp.zeros_like(d_im)
    msg_i[pl.ds(ROWS, RI - ROWS), :] = jnp.zeros((RI - ROWS, LANES), BF16)
    if RO > ROWS:
        msg_o[pl.ds(ROWS, RO - ROWS), :] = jnp.zeros((RO - ROWS, LANES), BF16)
    tsc[...] = jnp.zeros_like(tsc)
    scale_row[...] = scale_of(rate_row[...])
    mag = jnp.exp(-rate_t[...])
    lam = (mag * jnp.cos(rot_t[...]), mag * jnp.sin(rot_t[...]))
    lam_dev = cpow(lam, T)
    lam_plane = cpow(lam_dev, G)

    def widen(j):
        pad[pl.ds(8, T), cols(j)] = tok[:, cols(j)].astype(F32)
    loop(NP, widen)
    send_halo.wait()

    def lead(j):
        rows = halo[:, cols(j)].astype(F32)[8:]
        pad[pl.ds(0, 8), cols(j)] = jnp.where(me == 0, 0.0, rows)
    loop(NP, lead)

    def forward_in(j):
        conv = taps[pl.ds(0, 1), cols(j)] * pad[pl.ds(8, T), cols(j)]
        for k in range(1, KW):
            conv = conv + taps[pl.ds(k, 1), cols(j)] * pad[pl.ds(8 - k, T), cols(j)]
        x = conv.astype(BF16)
        mixed_in[:, cols(j)] = x
        drive = dot(x, w_in[j], 1, 0)
        scale = scale_row[:, cols(j)]
        d_re[pl.ds(j, T, PP), :] = drive[:, :LANES] * scale
        d_im[pl.ds(j, T, PP), :] = drive[:, LANES:] * scale
    loop(NP, forward_in)

    zero = jnp.zeros((PP, LANES), F32)
    STEP = 8

    def tile(t):
        return pl.ds(pl.multiple_of(t * PP, PP), PP)

    def run(re, im, write):
        def steps(b, carry):
            re, im, kp = carry
            for u in range(STEP):
                t = b * STEP + u
                k = keep[t]
                cr, ci = lam[0] * k, lam[1] * k
                xr, xi = d_re[tile(t), :], d_im[tile(t), :]
                re, im = (cr * re + xr) - ci * im, (cr * im + xi) + ci * re
                kp = kp * k
                if write:
                    d_re[tile(t), :] = re
                    d_im[tile(t), :] = im
            return re, im, kp
        return lax.fori_loop(0, T // STEP, steps, (re, im, jnp.ones((8, LANES), F32)))

    def run_back(re, im, write):
        def steps(b, carry):
            re, im = carry
            for u in range(STEP):
                t = T - 1 - (b * STEP + u)
                k = keep[t]
                cr, ci = lam[0] * k, lam[1] * k
                ar, ai = d_re[tile(t), :] + re, d_im[tile(t), :] + im
                if write:
                    d_re[tile(t), :] = ar
                    d_im[tile(t), :] = ai
                re, im = cr * ar + ci * ai, cr * ai - ci * ar
            return re, im
        return lax.fori_loop(0, T // STEP, steps, (re, im))

    def put(buf, value, k):
        buf[0, :PP, :] = value[0]
        buf[0, PP:2 * PP, :] = value[1]
        buf[0, 2 * PP:, :] = k

    def entry(buf, slot):
        return (buf[slot, :PP, :], buf[slot, PP:2 * PP, :]), buf[slot, pl.ds(2 * PP, 1), :]

    def fold(buf, place, count, step, init, all_too, back):
        order = range(count - 1, -1, -1) if back else range(count)
        c, total, kt = init, (zero, zero), jnp.ones((1, LANES), F32)
        for g in order:
            e, k = entry(buf, lax.rem(place - g + count, count))
            a = (step[0] * k, step[1] * k)
            m = cmul(a, c)
            use = (g > place) if back else (g < place)
            c = (jnp.where(use, m[0] + e[0], c[0]), jnp.where(use, m[1] + e[1], c[1]))
            if all_too:
                m = cmul(a, total)
                total = (m[0] + e[0], m[1] + e[1])
                kt = kt * k
        return c, total, kt

    def plane_start(buf, sems):
        copies = [remote(buf.at[0], buf.at[i], sems, i, plane(i)) for i in range(1, G)]
        for c in copies:
            c.start()
        return copies

    def z_start(buf, sems):
        copies = [remote(buf.at[0], buf.at[i], sems, i, along(i)) for i in range(1, Z)]
        for c in copies:
            c.start()
        return copies

    def wait(copies):
        for c in copies:
            c.wait()

    end_re, end_im, kprod = run(zero, zero, False)
    put(fb1, (end_re, end_im), kprod)
    wait(plane_start(fb1, s_f1))
    _, total, kt = fold(fb1, gi, G, lam_dev, (zero, zero), True, False)
    put(fb2, total, jnp.broadcast_to(kt, (8, LANES)))
    wait(z_start(fb2, s_f2))
    c, _, _ = fold(fb2, zi, Z, lam_plane, (zero, zero), False, False)
    c, _, _ = fold(fb1, gi, G, lam_dev, c, False, False)
    run(c[0], c[1], True)

    nbuf[0] = jnp.zeros((T, LANES), F32)
    half = lax.broadcasted_iota(jnp.int32, (T, LANES), 1) < HW

    def readout(j, carry):
        sq, dt = carry
        state = jnp.concatenate(
            [d_re[pl.ds(j, T, PP), :].astype(BF16), d_im[pl.ds(j, T, PP), :].astype(BF16)], axis=1)
        s_bf[:, cols(j, 2 * LANES)] = state
        m = dot(state, w_out[j], 1, 1) + skip[:, cols(j)] * mixed_in[:, cols(j)].astype(F32)
        mixed[:, cols(j)] = m
        scaled = cot[:, cols(j)].astype(F32) * gain[:, cols(j)]
        return sq + m * m, dt + scaled * m
    wide = jnp.zeros((T, LANES), F32)
    sq, dt = lax.fori_loop(0, NP, readout, (wide, wide))
    nbuf[0] = jnp.where(half, sq + pltpu.roll(sq, HW, 1), dt + pltpu.roll(dt, HW, 1))
    copies = [remote(nbuf.at[0], nbuf.at[i], s_norm, i, other(i)) for i in range(1, C)]
    for cp in copies:
        cp.start()
    wait(copies)
    both = nbuf[0]
    for i in range(1, C):
        both = both + nbuf[i]
    sq = jnp.sum(jnp.where(half, both, 0.0), axis=1, keepdims=True)
    dt = jnp.sum(jnp.where(half, 0.0, both), axis=1, keepdims=True)
    model = W * C
    inv = lax.rsqrt(sq / model + 1e-6)
    pull = inv * inv * dt / model

    def norm_back(j):
        m = mixed[:, cols(j)]
        g = gain[:, cols(j)]
        normed_o[:, cols(j)] = (m * inv * g).astype(BF16)
        scaled = cot[:, cols(j)].astype(F32) * g
        mg = inv * (scaled - m * pull)
        mixed[:, cols(j)] = mg
        gb = mg.astype(BF16)
        g_bf[:, cols(j)] = gb
        sg = dot(gb, w_out[j], 1, 0)
        d_re[pl.ds(j, T, PP), :] = sg[:, :LANES]
        d_im[pl.ds(j, T, PP), :] = sg[:, LANES:]
    loop(NP, norm_back)

    first = run_back(zero, zero, False)
    put(bb1, first, kprod)
    b1 = plane_start(bb1, s_b1)

    def out_grads(j):
        a, b = unpair(dot(g_bf[:, cols(j)], s_bf[:, cols(j, 2 * LANES)], 0, 0))
        msg_o[cols(2 * j, HW), :] = a.astype(BF16)
        msg_o[cols(2 * j + 1, HW), :] = b.astype(BF16)
    loop(NP, out_grads)

    conj_dev = (lam_dev[0], -lam_dev[1])
    conj_plane = (lam_plane[0], -lam_plane[1])
    wait(b1)
    _, total, kt = fold(bb1, gi, G, conj_dev, (zero, zero), True, True)
    put(bb2, total, jnp.broadcast_to(kt, (8, LANES)))
    b2 = z_start(bb2, s_b2)

    def chunk(i, size):
        return pl.ds(pl.multiple_of(i * size, 16), size)

    def sum1_start(msg, rs1, sems, rows):
        size = rows // G
        copies = [remote(msg.at[chunk(lax.rem(gi + i, G), size)], rs1.at[i], sems, i, plane(i))
                  for i in range(1, G)]
        for cp in copies:
            cp.start()
        return copies

    def sum1_end(copies, msg, rs1, mid, rows):
        wait(copies)
        size = rows // G
        total = msg[chunk(gi, size), :].astype(F32)
        for i in range(1, G):
            total = total + rs1[i].astype(F32)
        mid[...] = total.astype(BF16)

    def sum2_start(mid, rs2, sems, rows):
        size = rows // NSEQ
        copies = [remote(mid.at[chunk(lax.rem(zi + i, Z), size)], rs2.at[i], sems, i, along(i))
                  for i in range(1, Z)]
        for cp in copies:
            cp.start()
        return copies

    def sum2_end(copies, mid, rs2, res, rows):
        wait(copies)
        size = rows // NSEQ
        total = mid[chunk(zi, size), :].astype(F32)
        for i in range(1, Z):
            total = total + rs2[i].astype(F32)
        res[chunk(gi * Z + zi, size), :] = total.astype(BF16)

    def gather1_start(res, sems, rows):
        part = res.at[chunk(gi * Z + zi, rows // NSEQ)]
        copies = [remote(part, part, sems, i, along(i)) for i in range(1, Z)]
        for cp in copies:
            cp.start()
        return copies

    def gather2_start(res, sems, rows):
        part = res.at[chunk(gi, rows // G)]
        copies = [remote(part, part, sems, i, plane(i)) for i in range(1, G)]
        for cp in copies:
            cp.start()
        return copies

    o1 = sum1_start(msg_o, rs1_o, s_o1, RO)
    wait(b2)
    c, _, _ = fold(bb2, zi, Z, conj_plane, (zero, zero), False, True)
    c, _, _ = fold(bb1, gi, G, conj_dev, c, False, True)
    run_back(c[0], c[1], True)

    sum1_end(o1, msg_o, rs1_o, mid_o, RO)
    o2 = sum2_start(mid_o, rs2_o, s_o2, RO)

    def backward_in(j):
        scale = scale_row[:, cols(j)]
        dg = jnp.concatenate(
            [(d_re[pl.ds(j, T, PP), :] * scale).astype(BF16),
             (d_im[pl.ds(j, T, PP), :] * scale).astype(BF16)], axis=1)
        a, b = unpair(dot(mixed_in[:, cols(j)], dg, 0, 0))
        msg_i[cols(2 * j, HW), :] = a.astype(BF16)
        msg_i[cols(2 * j + 1, HW), :] = b.astype(BF16)
        g = dot(dg, w_in[j], 1, 1) + skip[:, cols(j)] * mixed[:, cols(j)]
        ig[pl.ds(0, T), cols(j)] = g
        for k in range(KW):
            tsc[pl.ds(k * NP + j, 1), :] = jnp.sum(
                g * pad[pl.ds(8 - k, T), cols(j)], axis=0, keepdims=True)
    loop(NP, backward_in)
    msg_i[pl.ds(ROWS, tsc.shape[0]), :] = tsc[...].astype(BF16)
    send_ig = remote(ig.at[pl.ds(0, 8)], ihalo, s_halo, 1, prv)
    send_ig.start()
    i1 = sum1_start(msg_i, rs1_i, s_i1, RI)

    sum2_end(o2, mid_o, rs2_o, res_o, RO)
    o3 = gather1_start(res_o, s_o3, RO)
    send_ig.wait()

    def token_grads(j):
        ig[pl.ds(T, 8), cols(j)] = jnp.where(me == NSEQ - 1, 0.0, ihalo[:, cols(j)])
        g = taps[pl.ds(0, 1), cols(j)] * ig[pl.ds(0, T), cols(j)]
        for k in range(1, KW):
            g = g + taps[pl.ds(k, 1), cols(j)] * ig[pl.ds(k, T), cols(j)]
        tg_o[:, cols(j)] = g.astype(BF16)
    loop(NP, token_grads)

    sum1_end(i1, msg_i, rs1_i, mid_i, RI)
    i2 = sum2_start(mid_i, rs2_i, s_i2, RI)
    wait(o3)
    o4 = gather2_start(res_o, s_o4, RO)
    sum2_end(i2, mid_i, rs2_i, res_i, RI)
    i3 = gather1_start(res_i, s_i3, RI)

    def widen_out(res, out):
        def one(h):
            out[h] = res[cols(h, HW), :].astype(F32)
        loop(ROWS // HW, one)

    wait(i3)
    i4 = gather2_start(res_i, s_i4, RI)
    wait(o4)
    widen_out(res_o, out_o)
    wait(i4)
    widen_out(res_i, in_o)
    tsc[...] = res_i[pl.ds(ROWS, tsc.shape[0]), :].astype(F32)

    def put_taps(j):
        for k in range(KW):
            taps_o[pl.ds(k, 1), cols(j)] = tsc[pl.ds(k * NP + j, 1), :]
    loop(NP, put_taps)


def up(value, unit):
    return -(-value // unit) * unit


def per_device(num_seq, num_chan, tokens, conv_taps, log_rate, rotation, in_proj, out_proj,
               skip_gain, norm_gain, retention, cotangent):
    T, W = tokens.shape
    KW = conv_taps.shape[0]
    NH, HW, K2 = in_proj.shape
    NP = NH // 2
    PP = up(NP, 8)
    G = 1
    while G * G < num_seq:
        G *= 2
    Z = num_seq // G
    ROWS = NH * HW
    TP = up(KW * NP, 16)
    RO = up(ROWS, num_seq * 16)
    RI = up(ROWS + TP, num_seq * 16)
    dims = (T, W, NP, PP, KW, HW, G, Z, num_chan, num_seq, ROWS, RO, RI)

    def tiled(x):
        x = x.reshape(NP, LANES)
        return jnp.pad(x, ((0, PP - NP), (0, 0))) if PP != NP else x

    row = lambda x: x.reshape(1, W)
    vm = pl.BlockSpec(memory_space=pltpu.VMEM)
    sm = pl.BlockSpec(memory_space=pltpu.SMEM)
    V = pltpu.VMEM
    M = 2 * PP + 8
    sem = lambda n: pltpu.SemaphoreType.DMA((2, n))

    def bufs(rows):
        return [V((rows, LANES), BF16), V((G, rows // G, LANES), BF16), V((rows // G, LANES), BF16),
                V((Z, rows // num_seq, LANES), BF16), V((rows, LANES), BF16)]

    scratch = [
        V((T + 8, W), F32), V((T, W), BF16), V((T * PP, LANES), F32), V((T * PP, LANES), F32),
        V((T, 2 * W), BF16), V((T, W), F32), V((T, W), BF16), V((T + 8, W), F32),
        V((NP, 2 * HW, 2 * LANES), BF16), V((NP, 2 * HW, 2 * LANES), BF16), V((1, W), F32),
        V((TP, LANES), F32), V((16, W), BF16), V((8, W), F32),
        V((num_chan, T, LANES), F32),
        V((G, M, LANES), F32), V((Z, M, LANES), F32), V((G, M, LANES), F32), V((Z, M, LANES), F32),
        *bufs(RO), *bufs(RI),
        sem(2), sem(num_chan), sem(G), sem(Z), sem(G), sem(Z),
        sem(G), sem(Z), sem(Z), sem(G), sem(G), sem(Z), sem(Z), sem(G),
    ]
    S = jax.ShapeDtypeStruct
    return pl.pallas_call(
        functools.partial(kernel, dims),
        out_shape=(S((T, W), BF16), S((T, W), BF16), S((NH, HW, K2), F32), S((NH, HW, K2), F32),
                   S((KW, W), F32)),
        in_specs=[vm] * 10 + [sm],
        out_specs=(vm,) * 5,
        scratch_shapes=scratch,
        compiler_params=pltpu.CompilerParams(
            collective_id=0, has_side_effects=True, vmem_limit_bytes=48 * 1024 * 1024),
    )(tokens, conv_taps, row(log_rate), tiled(log_rate), tiled(rotation), in_proj, out_proj,
      row(skip_gain), row(norm_gain), cotangent, retention)


def solution(mesh):
    in_specs = (
        P("seq", "chan"), P(None, "chan"), P("chan"), P("chan"), P("chan", None, None),
        P("chan", None, None), P("chan"), P("chan"), P("seq"), P("seq", "chan"),
    )
    out_specs = (
        P("seq", "chan"), P("seq", "chan"), P("chan", None, None), P("chan", None, None),
        P(None, "chan"),
    )
    body = functools.partial(per_device, mesh.shape["seq"], mesh.shape["chan"])
    return jax.shard_map(body, mesh=mesh, in_specs=in_specs, out_specs=out_specs, check_vma=False)
```

```python
import functools

import jax
import jax.numpy as jnp
from jax import lax
from jax.experimental import pallas as pl
from jax.experimental.pallas import tpu as pltpu
from jax.sharding import PartitionSpec as P

LANES = 128
F32 = jnp.float32
BF16 = jnp.bfloat16


def cmul(a, b):
    return a[0] * b[0] - a[1] * b[1], a[0] * b[1] + a[1] * b[0]


def cpow(base, exponent):
    result = None
    while exponent:
        if exponent & 1:
            result = base if result is None else cmul(result, base)
        exponent >>= 1
        if exponent:
            base = cmul(base, base)
    return result


def dot(a, b, ca, cb):
    return lax.dot_general(a, b, (((ca,), (cb,)), ((), ())), preferred_element_type=F32)


def scale_of(rate):
    sq = rate * rate
    sinh = rate * (1 + sq / 6 * (1 + sq / 20 * (1 + sq / 42 * (1 + sq / 72))))
    return jnp.sqrt(2.0 * jnp.exp(-rate) * sinh)


def kernel(dims, *refs):
    (tok_h, taps_h, rate_row_h, rate_t_h, rot_t_h, win_h, wout_h, skip_h, gain_h, cot_h, keep,
     normed_o, tg_o, res_o, res_i, taps_o,
     tok, taps, rate_row, rate_t, rot_t, win, wout, skip, gain, cot, s_in,
     pad, mixed_in, d_re, d_im, s_bf, mixed, g_bf, ig, w_in, w_out, scale_row, tsc, halo, ihalo,
     nbuf, fb1, fb2, bb1, bb2, msg_o, rs1_o, mid_o, rs2_o,
     msg_i, rs1_i, mid_i, rs2_i,
     s_halo, s_norm, s_f1, s_f2, s_b1, s_b2, s_o1, s_o2, s_o3, s_o4, s_i1, s_i2, s_i3, s_i4) = refs
    T, W, NP, PP, KW, HW, G, Z, C, NSEQ, ROWS, RO, RI = dims
    me = lax.axis_index("seq")
    core = lax.axis_index("chan")
    gi = lax.rem(me, G)
    zi = me // G

    def plane(i):
        return {"seq": zi * G + lax.rem(gi + i, G)}

    def along(i):
        return {"seq": lax.rem(zi + i, Z) * G + gi}

    def other(i):
        return {"chan": lax.rem(core + i, C)}

    nxt = {"seq": lax.rem(me + 1, NSEQ)}
    prv = {"seq": lax.rem(me + NSEQ - 1, NSEQ)}

    peers = [plane(i) for i in range(1, G)] + [along(i) for i in range(1, Z)]
    peers += [other(i) for i in range(1, C)] + [nxt, prv]
    barrier = pltpu.get_barrier_semaphore()
    for peer in peers:
        pl.semaphore_signal(barrier, inc=1, device_id=peer, device_id_type=pl.DeviceIdType.MESH)

    pairs = [(tok_h, tok), (win_h, win), (taps_h, taps), (rate_row_h, rate_row),
             (rate_t_h, rate_t), (rot_t_h, rot_t), (wout_h, wout), (skip_h, skip),
             (gain_h, gain), (cot_h, cot)]
    loads = [pltpu.make_async_copy(src, dst, s_in.at[i]) for i, (src, dst) in enumerate(pairs)]
    for cp in loads:
        cp.start()

    def remote(src, dst, sems, i, device):
        return pltpu.make_async_remote_copy(
            src_ref=src, dst_ref=dst, send_sem=sems.at[0, i], recv_sem=sems.at[1, i],
            device_id=device, device_id_type=pl.DeviceIdType.MESH,
        )

    def loop(count, body):
        unroll = 4 if count % 4 == 0 else 1

        def several(i, _):
            for u in range(unroll):
                body(i * unroll + u)
        lax.fori_loop(0, count // unroll, several, None)

    def cols(j, width=LANES):
        return pl.ds(pl.multiple_of(j * width, width), width)

    low = lax.broadcasted_iota(jnp.int32, (HW, LANES), 1) < HW

    def pair_weights(src, dst):
        def one(j):
            a = src[2 * j].astype(F32)
            b = src[2 * j + 1].astype(F32)
            ar = pltpu.roll(a, HW, 1)
            br = pltpu.roll(b, HW, 1)
            dst[j, :HW, :LANES] = jnp.where(low, a, 0.0).astype(BF16)
            dst[j, HW:, :LANES] = jnp.where(low, 0.0, br).astype(BF16)
            dst[j, :HW, LANES:] = jnp.where(low, ar, 0.0).astype(BF16)
            dst[j, HW:, LANES:] = jnp.where(low, 0.0, b).astype(BF16)
        loop(NP, one)

    def unpair(r):
        top_re, top_im = r[:HW, :LANES], r[:HW, LANES:]
        bot_re, bot_im = r[HW:, :LANES], r[HW:, LANES:]
        a = jnp.where(low, top_re, pltpu.roll(top_im, HW, 1))
        b = jnp.where(low, pltpu.roll(bot_re, HW, 1), bot_im)
        return a, b

    for cp in loads[1:6]:
        cp.wait()
    pair_weights(win, w_in)
    scale_row[...] = scale_of(rate_row[...])
    mag = jnp.exp(-rate_t[...])
    lam = (mag * jnp.cos(rot_t[...]), mag * jnp.sin(rot_t[...]))
    lam_dev = cpow(lam, T)
    lam_plane = cpow(lam_dev, G)
    pl.semaphore_wait(barrier, len(peers))
    send_halo = remote(tok_h.at[pl.ds(T - 16, 16)], halo, s_halo, 0, nxt)
    send_halo.start()
    loads[0].wait()

    if PP != NP:
        d_re[...] = jnp.zeros_like(d_re)
        d_im[...] = jnp.zeros_like(d_im)

    def widen(j):
        pad[pl.ds(8, T), cols(j)] = tok[:, cols(j)].astype(F32)
    loop(NP, widen)
    send_halo.wait()

    def lead(j):
        rows = halo[:, cols(j)].astype(F32)[8:]
        pad[pl.ds(0, 8), cols(j)] = jnp.where(me == 0, 0.0, rows)
    loop(NP, lead)

    def forward_in(j):
        conv = taps[pl.ds(0, 1), cols(j)] * pad[pl.ds(8, T), cols(j)]
        for k in range(1, KW):
            conv = conv + taps[pl.ds(k, 1), cols(j)] * pad[pl.ds(8 - k, T), cols(j)]
        x = conv.astype(BF16)
        mixed_in[:, cols(j)] = x
        drive = dot(x, w_in[j], 1, 0)
        scale = scale_row[:, cols(j)]
        d_re[pl.ds(j, T, PP), :] = drive[:, :LANES] * scale
        d_im[pl.ds(j, T, PP), :] = drive[:, LANES:] * scale
    loop(NP, forward_in)

    zero = jnp.zeros((PP, LANES), F32)
    STEP = 8

    def tile(t):
        return pl.ds(pl.multiple_of(t * PP, PP), PP)

    def run(re, im, write):
        def steps(b, carry):
            re, im, kp = carry
            for u in range(STEP):
                t = b * STEP + u
                k = keep[t]
                cr, ci = lam[0] * k, lam[1] * k
                xr, xi = d_re[tile(t), :], d_im[tile(t), :]
                re, im = (cr * re + xr) - ci * im, (cr * im + xi) + ci * re
                kp = kp * k
                if write:
                    d_re[tile(t), :] = re
                    d_im[tile(t), :] = im
            return re, im, kp
        return lax.fori_loop(0, T // STEP, steps, (re, im, jnp.ones((8, LANES), F32)))

    def run_back(re, im, write):
        def steps(b, carry):
            re, im = carry
            for u in range(STEP):
                t = T - 1 - (b * STEP + u)
                k = keep[t]
                cr, ci = lam[0] * k, lam[1] * k
                ar, ai = d_re[tile(t), :] + re, d_im[tile(t), :] + im
                if write:
                    d_re[tile(t), :] = ar
                    d_im[tile(t), :] = ai
                re, im = cr * ar + ci * ai, cr * ai - ci * ar
            return re, im
        return lax.fori_loop(0, T // STEP, steps, (re, im))

    def put(buf, value, k):
        buf[0, :PP, :] = value[0]
        buf[0, PP:2 * PP, :] = value[1]
        buf[0, 2 * PP:, :] = k

    def entry(buf, slot):
        return (buf[slot, :PP, :], buf[slot, PP:2 * PP, :]), buf[slot, pl.ds(2 * PP, 1), :]

    def fold(buf, place, count, step, init, all_too, back):
        order = range(count - 1, -1, -1) if back else range(count)
        c, total, kt = init, (zero, zero), jnp.ones((1, LANES), F32)
        for g in order:
            e, k = entry(buf, lax.rem(place - g + count, count))
            a = (step[0] * k, step[1] * k)
            m = cmul(a, c)
            use = (g > place) if back else (g < place)
            c = (jnp.where(use, m[0] + e[0], c[0]), jnp.where(use, m[1] + e[1], c[1]))
            if all_too:
                m = cmul(a, total)
                total = (m[0] + e[0], m[1] + e[1])
                kt = kt * k
        return c, total, kt

    def plane_start(buf, sems):
        copies = [remote(buf.at[0], buf.at[i], sems, i, plane(i)) for i in range(1, G)]
        for c in copies:
            c.start()
        return copies

    def z_start(buf, sems):
        copies = [remote(buf.at[0], buf.at[i], sems, i, along(i)) for i in range(1, Z)]
        for c in copies:
            c.start()
        return copies

    def wait(copies):
        for c in copies:
            c.wait()

    end_re, end_im, kprod = run(zero, zero, False)
    put(fb1, (end_re, end_im), kprod)
    f1 = plane_start(fb1, s_f1)
    for cp in loads[6:]:
        cp.wait()
    pair_weights(wout, w_out)
    msg_i[pl.ds(ROWS, RI - ROWS), :] = jnp.zeros((RI - ROWS, LANES), BF16)
    if RO > ROWS:
        msg_o[pl.ds(ROWS, RO - ROWS), :] = jnp.zeros((RO - ROWS, LANES), BF16)
    tsc[...] = jnp.zeros_like(tsc)
    wait(f1)
    _, total, kt = fold(fb1, gi, G, lam_dev, (zero, zero), True, False)
    put(fb2, total, jnp.broadcast_to(kt, (8, LANES)))
    wait(z_start(fb2, s_f2))
    c, _, _ = fold(fb2, zi, Z, lam_plane, (zero, zero), False, False)
    c, _, _ = fold(fb1, gi, G, lam_dev, c, False, False)
    run(c[0], c[1], True)

    half = lax.broadcasted_iota(jnp.int32, (T, LANES), 1) < HW

    def readout_one(j, carry):
        sq, dt = carry
        state = jnp.concatenate(
            [d_re[pl.ds(j, T, PP), :].astype(BF16), d_im[pl.ds(j, T, PP), :].astype(BF16)], axis=1)
        s_bf[:, cols(j, 2 * LANES)] = state
        m = dot(state, w_out[j], 1, 1) + skip[:, cols(j)] * mixed_in[:, cols(j)].astype(F32)
        mixed[:, cols(j)] = m
        scaled = cot[:, cols(j)].astype(F32) * gain[:, cols(j)]
        return sq + m * m, dt + scaled * m
    runs = 4 if NP % 4 == 0 else 1

    def readout(i, carry):
        for u in range(runs):
            carry = readout_one(i * runs + u, carry)
        return carry
    wide = jnp.zeros((T, LANES), F32)
    sq, dt = lax.fori_loop(0, NP // runs, readout, (wide, wide))
    nbuf[0] = jnp.where(half, sq + pltpu.roll(sq, HW, 1), dt + pltpu.roll(dt, HW, 1))
    copies = [remote(nbuf.at[0], nbuf.at[i], s_norm, i, other(i)) for i in range(1, C)]
    for cp in copies:
        cp.start()
    wait(copies)
    both = nbuf[0]
    for i in range(1, C):
        both = both + nbuf[i]
    sq = jnp.sum(jnp.where(half, both, 0.0), axis=1, keepdims=True)
    dt = jnp.sum(jnp.where(half, 0.0, both), axis=1, keepdims=True)
    model = W * C
    inv = lax.rsqrt(sq / model + 1e-6)
    pull = inv * inv * dt / model

    def norm_back(j):
        m = mixed[:, cols(j)]
        g = gain[:, cols(j)]
        normed_o[:, cols(j)] = (m * inv * g).astype(BF16)
        scaled = cot[:, cols(j)].astype(F32) * g
        mg = inv * (scaled - m * pull)
        mixed[:, cols(j)] = mg
        gb = mg.astype(BF16)
        g_bf[:, cols(j)] = gb
        sg = dot(gb, w_out[j], 1, 0)
        d_re[pl.ds(j, T, PP), :] = sg[:, :LANES]
        d_im[pl.ds(j, T, PP), :] = sg[:, LANES:]
    loop(NP, norm_back)

    first = run_back(zero, zero, False)
    put(bb1, first, kprod)
    b1 = plane_start(bb1, s_b1)

    def out_grads(j):
        a, b = unpair(dot(g_bf[:, cols(j)], s_bf[:, cols(j, 2 * LANES)], 0, 0))
        msg_o[cols(2 * j, HW), :] = a.astype(BF16)
        msg_o[cols(2 * j + 1, HW), :] = b.astype(BF16)
    loop(NP, out_grads)

    conj_dev = (lam_dev[0], -lam_dev[1])
    conj_plane = (lam_plane[0], -lam_plane[1])
    wait(b1)
    _, total, kt = fold(bb1, gi, G, conj_dev, (zero, zero), True, True)
    put(bb2, total, jnp.broadcast_to(kt, (8, LANES)))
    b2 = z_start(bb2, s_b2)

    def chunk(i, size):
        return pl.ds(pl.multiple_of(i * size, 16), size)

    def sum1_start(msg, rs1, sems, rows):
        size = rows // G
        copies = [remote(msg.at[chunk(lax.rem(gi + i, G), size)], rs1.at[i], sems, i, plane(i))
                  for i in range(1, G)]
        for cp in copies:
            cp.start()
        return copies

    def sum1_end(copies, msg, rs1, mid, rows):
        wait(copies)
        size = rows // G
        total = msg[chunk(gi, size), :].astype(F32)
        for i in range(1, G):
            total = total + rs1[i].astype(F32)
        mid[...] = total.astype(BF16)

    def sum2_start(mid, rs2, sems, rows):
        size = rows // NSEQ
        copies = [remote(mid.at[chunk(lax.rem(zi + i, Z), size)], rs2.at[i], sems, i, along(i))
                  for i in range(1, Z)]
        for cp in copies:
            cp.start()
        return copies

    def sum2_end(copies, mid, rs2, res, rows):
        wait(copies)
        size = rows // NSEQ
        total = mid[chunk(zi, size), :].astype(F32)
        for i in range(1, Z):
            total = total + rs2[i].astype(F32)
        res[chunk(gi * Z + zi, size), :] = total.astype(BF16)

    def gather1_start(res, sems, rows):
        part = res.at[chunk(gi * Z + zi, rows // NSEQ)]
        copies = [remote(part, part, sems, i, along(i)) for i in range(1, Z)]
        for cp in copies:
            cp.start()
        return copies

    def gather2_start(res, sems, rows):
        part = res.at[chunk(gi, rows // G)]
        copies = [remote(part, part, sems, i, plane(i)) for i in range(1, G)]
        for cp in copies:
            cp.start()
        return copies

    o1 = sum1_start(msg_o, rs1_o, s_o1, RO)
    wait(b2)
    c, _, _ = fold(bb2, zi, Z, conj_plane, (zero, zero), False, True)
    c, _, _ = fold(bb1, gi, G, conj_dev, c, False, True)
    run_back(c[0], c[1], True)

    def backward_in(j):
        scale = scale_row[:, cols(j)]
        dg = jnp.concatenate(
            [(d_re[pl.ds(j, T, PP), :] * scale).astype(BF16),
             (d_im[pl.ds(j, T, PP), :] * scale).astype(BF16)], axis=1)
        a, b = unpair(dot(mixed_in[:, cols(j)], dg, 0, 0))
        msg_i[cols(2 * j, HW), :] = a.astype(BF16)
        msg_i[cols(2 * j + 1, HW), :] = b.astype(BF16)
        g = dot(dg, w_in[j], 1, 1) + skip[:, cols(j)] * mixed[:, cols(j)]
        ig[pl.ds(0, T), cols(j)] = g
        for k in range(KW):
            tsc[pl.ds(k * NP + j, 1), :] = jnp.sum(
                g * pad[pl.ds(8 - k, T), cols(j)], axis=0, keepdims=True)
    loop(NP, backward_in)
    msg_i[pl.ds(ROWS, tsc.shape[0]), :] = tsc[...].astype(BF16)
    send_ig = remote(ig.at[pl.ds(0, 8)], ihalo, s_halo, 1, prv)
    send_ig.start()
    i1 = sum1_start(msg_i, rs1_i, s_i1, RI)
    sum1_end(o1, msg_o, rs1_o, mid_o, RO)
    o2 = sum2_start(mid_o, rs2_o, s_o2, RO)

    sum2_end(o2, mid_o, rs2_o, res_o, RO)
    o3 = gather1_start(res_o, s_o3, RO)
    send_ig.wait()

    def token_grads(j):
        ig[pl.ds(T, 8), cols(j)] = jnp.where(me == NSEQ - 1, 0.0, ihalo[:, cols(j)])
        g = taps[pl.ds(0, 1), cols(j)] * ig[pl.ds(0, T), cols(j)]
        for k in range(1, KW):
            g = g + taps[pl.ds(k, 1), cols(j)] * ig[pl.ds(k, T), cols(j)]
        tg_o[:, cols(j)] = g.astype(BF16)
    loop(NP, token_grads)

    sum1_end(i1, msg_i, rs1_i, mid_i, RI)
    i2 = sum2_start(mid_i, rs2_i, s_i2, RI)
    wait(o3)
    o4 = gather2_start(res_o, s_o4, RO)
    sum2_end(i2, mid_i, rs2_i, res_i, RI)
    i3 = gather1_start(res_i, s_i3, RI)

    wait(i3)
    i4 = gather2_start(res_i, s_i4, RI)
    wait(o4)
    wait(i4)
    tsc[...] = res_i[pl.ds(ROWS, tsc.shape[0]), :].astype(F32)

    def put_taps(j):
        for k in range(KW):
            taps_o[pl.ds(k, 1), cols(j)] = tsc[pl.ds(k * NP + j, 1), :]
    loop(NP, put_taps)


def finish(dims, normed, tg, res_o, res_i, taps, normed_h, tg_h, in_h, out_h, taps_h,
           wide_o, wide_i, sems):
    NH, HW, PARTS = dims
    copies = []

    def put(src, dst):
        copies.append(pltpu.make_async_copy(src, dst, sems.at[len(copies)]))
        copies[-1].start()
    put(normed, normed_h)
    put(tg, tg_h)
    put(taps, taps_h)
    step = NH // PARTS
    for res, wide, out in ((res_o, wide_o, out_h), (res_i, wide_i, in_h)):
        for p in range(PARTS):
            for h in range(p * step, (p + 1) * step):
                wide[h] = res[pl.ds(h * HW, HW), :].astype(F32)
            put(wide.at[pl.ds(p * step, step)], out.at[pl.ds(p * step, step)])
    for cp in copies:
        cp.wait()


def up(value, unit):
    return -(-value // unit) * unit


def per_device(num_seq, num_chan, tokens, conv_taps, log_rate, rotation, in_proj, out_proj,
               skip_gain, norm_gain, retention, cotangent):
    T, W = tokens.shape
    KW = conv_taps.shape[0]
    NH, HW, K2 = in_proj.shape
    NP = NH // 2
    PP = up(NP, 8)
    G = 1
    while G * G < num_seq:
        G *= 2
    Z = num_seq // G
    ROWS = NH * HW
    TP = up(KW * NP, 16)
    RO = up(ROWS, num_seq * 16)
    RI = up(ROWS + TP, num_seq * 16)
    dims = (T, W, NP, PP, KW, HW, G, Z, num_chan, num_seq, ROWS, RO, RI)

    def tiled(x):
        x = x.reshape(NP, LANES)
        return jnp.pad(x, ((0, PP - NP), (0, 0))) if PP != NP else x

    row = lambda x: x.reshape(1, W)
    vm = pl.BlockSpec(memory_space=pltpu.VMEM)
    sm = pl.BlockSpec(memory_space=pltpu.SMEM)
    hb = pl.BlockSpec(memory_space=pltpu.HBM)
    V = pltpu.VMEM
    M = 2 * PP + 8
    sem = lambda n: pltpu.SemaphoreType.DMA((2, n))

    def bufs(rows):
        return [V((rows, LANES), BF16), V((G, rows // G, LANES), BF16), V((rows // G, LANES), BF16),
                V((Z, rows // num_seq, LANES), BF16)]

    scratch = [
        V((T, W), BF16), V((KW, W), F32), V((1, W), F32), V((PP, LANES), F32), V((PP, LANES), F32),
        V((NH, HW, K2), BF16), V((NH, HW, K2), BF16), V((1, W), F32), V((1, W), F32), V((T, W), BF16),
        pltpu.SemaphoreType.DMA((10,)),
        V((T + 8, W), F32), V((T, W), BF16), V((T * PP, LANES), F32), V((T * PP, LANES), F32),
        V((T, 2 * W), BF16), V((T, W), F32), V((T, W), BF16), V((T + 8, W), F32),
        V((NP, 2 * HW, 2 * LANES), BF16), V((NP, 2 * HW, 2 * LANES), BF16), V((1, W), F32),
        V((TP, LANES), F32), V((16, W), BF16), V((8, W), F32),
        V((num_chan, T, LANES), F32),
        V((G, M, LANES), F32), V((Z, M, LANES), F32), V((G, M, LANES), F32), V((Z, M, LANES), F32),
        *bufs(RO), *bufs(RI),
        sem(2), sem(num_chan), sem(G), sem(Z), sem(G), sem(Z),
        sem(G), sem(Z), sem(Z), sem(G), sem(G), sem(Z), sem(Z), sem(G),
    ]
    S = jax.ShapeDtypeStruct
    normed, tg, res_o, res_i, taps = pl.pallas_call(
        functools.partial(kernel, dims),
        out_shape=(S((T, W), BF16), S((T, W), BF16), S((RO, LANES), BF16), S((RI, LANES), BF16),
                   S((KW, W), F32)),
        in_specs=[hb] * 10 + [sm],
        out_specs=(vm,) * 5,
        scratch_shapes=scratch,
        compiler_params=pltpu.CompilerParams(
            collective_id=0, has_side_effects=True, vmem_limit_bytes=48 * 1024 * 1024),
    )(tokens, conv_taps, row(log_rate), tiled(log_rate), tiled(rotation), in_proj, out_proj,
      row(skip_gain), row(norm_gain), cotangent, retention)
    parts = 4
    return pl.pallas_call(
        functools.partial(finish, (NH, HW, parts)),
        out_shape=(S((T, W), BF16), S((T, W), BF16), S((NH, HW, K2), F32), S((NH, HW, K2), F32),
                   S((KW, W), F32)),
        in_specs=[vm] * 5,
        out_specs=(hb,) * 5,
        scratch_shapes=[V((NH, HW, K2), F32), V((NH, HW, K2), F32),
                        pltpu.SemaphoreType.DMA((3 + 2 * parts,))],
        compiler_params=pltpu.CompilerParams(vmem_limit_bytes=16 * 1024 * 1024),
    )(normed, tg, res_o, res_i, taps)


def solution(mesh):
    in_specs = (
        P("seq", "chan"), P(None, "chan"), P("chan"), P("chan"), P("chan", None, None),
        P("chan", None, None), P("chan"), P("chan"), P("seq"), P("seq", "chan"),
    )
    out_specs = (
        P("seq", "chan"), P("seq", "chan"), P("chan", None, None), P("chan", None, None),
        P(None, "chan"),
    )
    body = functools.partial(per_device, mesh.shape["seq"], mesh.shape["chan"])
    return jax.shard_map(body, mesh=mesh, in_specs=in_specs, out_specs=out_specs, check_vma=False)
```
